32 devices in a mesh: slab: 8 (over z, y), case: 4 (over x, core).
Axes of the slice: x: 2, y: 2, z: 4, core: 2. Of those that a mesh axis runs over, the one named last changes fastest.
Arguments:
- pressure: float32 [64, 512], replicated, may hold values from -9 to 9
- panel: int32 [96, 4, 128], P('slab'), may hold values from 0 to 511
- flags: int32 [96, 4, 128], P('slab'), may hold values 0 or 1
- diagonal: float32 [96, 4, 128], P('slab'), may hold values from 0.25 to 4
Outputs:
- fields: float32 [64, 96, 4, 128], P('case', 'slab')
- gram: float32 [64, 64], P('case')
- cross: float32 [64, 64], P('case')
The draws below stay inside these ranges and needn't reach their ends.
All inputs are finite; a program needn't handle non-finite values. No bound on the sum of `flags` on one device may be relied on, other than what follows from the above.
Results may differ from the reference program's by a relative error of at most 0.00005.
Values sent between devices are 32-bit elements; how exact they have to be, the bound alone decides.
No kernel may reach another device: no remote copies, remote signals or barrier semaphores. Data moves between devices by JAX's collectives and lax.ppermute only.
A program may use at most 64 MiB of HBM per device.

```python
import math
import jax
import jax.numpy as jnp
from jax import lax

NR = 4
NC = 128
NCASE = 64
PANELS = 512
NA = 96


def draw_pressure(key, part):
    first_key, second_key, third_key = jax.random.split(key, 3)
    amplitude = jax.random.uniform(first_key, (NCASE, 1), jnp.float32, 0.5, 1.5)
    pattern = jnp.clip(jax.random.normal(second_key, (1, PANELS), jnp.float32), -4.0, 4.0)
    variation = 0.7 * jnp.clip(jax.random.normal(third_key, (NCASE, PANELS), jnp.float32), -4.0, 4.0)
    return amplitude * pattern + variation


def place_ends(entries, rng, least, largest):
    longest = entries.shape.index(max(entries.shape))
    spots = []
    for shift in (0, 1):
        where = [jax.random.randint(jax.random.fold_in(rng, axis), (), 0, length) for axis, length in enumerate(entries.shape)]
        where[longest] = (where[longest] + shift) % entries.shape[longest]
        spots.append(tuple(where))
    return entries.at[spots[0]].set(least).at[spots[1]].set(largest)


def levels(own_key, extent, pieces, low, high):
    loudness, own = 1.0, jax.random.fold_in(own_key, 6)
    for position, blocks in pieces:
        draws = jnp.exp(jax.random.uniform(jax.random.fold_in(own, position), (blocks,), jnp.float32, low / len(pieces), high / len(pieces)))
        loudness = loudness * jnp.repeat(draws, extent[position] // blocks).reshape([-1 if axis == position else 1 for axis in range(len(extent))])
    return loudness


def setup_inputs(seed: int = 0) -> dict:
    key_of = jax.random.split(jax.random.key(seed), 5)
    return {
        "pressure": draw_pressure(jax.random.fold_in(key_of[4], 71), 0),
        "panel": place_ends(jax.random.randint(key_of[1], (NA, NR, NC), 0, PANELS), jax.random.fold_in(key_of[1], 1), 0, PANELS - 1).astype(jnp.int32),
        "flags": place_ends((jax.random.randint(key_of[2], (NA, NR, NC), 0, 8) < 1).astype(jnp.int32), jax.random.fold_in(key_of[2], 1), 0, 1),
        "diagonal": jnp.clip(jnp.exp(math.log(4.0) - 2.7725887 * jax.random.uniform(key_of[3], (NA, NR, NC), jnp.float32) ** levels(key_of[3], (NA, NR, NC), ((0, 8),), -0.2, 0.2)), 0.25, 4.0),
    }


damping = 0.7
penalty = 4.0
highest = lax.Precision.HIGHEST


def transverse(field):
    beside_all = jnp.roll(field, 1, axis=-1) + jnp.roll(field, -1, axis=-1)
    zero_row = jnp.zeros_like(field[..., :1, :])
    inward = jnp.concatenate([zero_row, field[..., :-1, :]], axis=-2)
    outward = jnp.concatenate([field[..., 1:, :], zero_row], axis=-2)
    return beside_all + inward + outward


def stencil(field, below, above, coeff, weight):
    return (coeff + 2.0 * weight + 4.0) * field - weight * (below + above) - transverse(field)


def apply_local(field, coeff, weight):
    zero_layer = jnp.zeros_like(field[:, :1])
    below = jnp.concatenate([zero_layer, field[:, :-1]], axis=1)
    above = jnp.concatenate([field[:, 1:], zero_layer], axis=1)
    return stencil(field, below, above, coeff, weight)


def smooth_local(field, rhs, coeff, weight):
    return field + damping * (rhs - apply_local(field, coeff, weight)) / (coeff + 2.0 * weight + 4.0)


def restrict(fine):
    even = fine[:, 0::2]
    odd = fine[:, 1::2]
    odd_before = jnp.concatenate([jnp.zeros_like(odd[:, :1]), odd[:, :-1]], axis=1)
    return 0.5 * even + 0.25 * (odd + odd_before)


def prolong(coarse):
    following = jnp.concatenate([coarse[:, 1:], jnp.zeros_like(coarse[:, :1])], axis=1)
    middle = 0.5 * (coarse + following)
    stacked = jnp.stack([coarse, middle], axis=2)
    shape = coarse.shape
    return stacked.reshape(shape[0], 2 * shape[1], shape[2], shape[3])


def vcycle(rhs, coeff, level):
    weight = 0.25 ** level
    field = damping * rhs / (coeff + 2.0 * weight + 4.0)
    if level == 2:
        for sweep in range(3):
            field = smooth_local(field, rhs, coeff, weight)
        return field
    field = smooth_local(field, rhs, coeff, weight)
    leftover = rhs - apply_local(field, coeff, weight)
    coarse_coeff = 0.5 * (coeff[0::2] + coeff[1::2])
    field = field + prolong(vcycle(restrict(leftover), coarse_coeff, level + 1))
    for sweep in range(2):
        field = smooth_local(field, rhs, coeff, weight)
    return field


def reference(pressure, panel, flags, diagonal):
    coeff = diagonal + penalty * flags.astype(jnp.float32)
    keep = 1.0 - flags.astype(jnp.float32)
    positions = jnp.arange(NA).astype(jnp.float32)
    span = (1.0 + 2.0 * positions / NA)[:, None, None]

    def one_case(load_row):
        rhs = jnp.take(load_row, panel.astype(jnp.int32), axis=0) * span * keep
        rhs = rhs[None]
        field = vcycle(rhs, coeff, 0)
        image = apply_local(field, coeff, 1.0)
        return field[0], image[0], rhs[0]

    fields, images, loads = lax.map(one_case, pressure)
    scale = 1.0 / (NA * NR * NC)
    fields_flat = fields.reshape(NCASE, -1)
    gram = jnp.dot(images.reshape(NCASE, -1), fields_flat.T, precision=highest, preferred_element_type=jnp.float32) * scale
    cross = jnp.dot(loads.reshape(NCASE, -1), fields_flat.T, precision=highest, preferred_element_type=jnp.float32) * scale
    return (fields, gram, cross)
```

```python
import functools

import jax
import jax.numpy as jnp
from jax import lax
from jax.experimental import pallas as pl
from jax.experimental.pallas import tpu as pltpu
from jax.sharding import PartitionSpec as P

damping = 0.7
penalty = 4.0
f32 = jnp.float32
bf16 = jnp.bfloat16
SUB = 8
REACH = 32
BELOW, ABOVE = 29, 30


def over(lo, hi, step, body):
    count = hi - lo + 1
    whole = count // step
    if whole > 1:

        def trip(i, carry):
            body(lo + i * step, step)
            return carry

        lax.fori_loop(0, whole, trip, 0)
    elif whole == 1:
        body(lo, step)
    if count - whole * step:
        body(lo + whole * step, count - whole * step)


def cycle_kernel(
    meta, table, panel, flags, diagonal, *refs, tiles, own_tiles, n, total, R, hops
):
    mine, theirs = refs[:hops], refs[hops : 2 * hops]
    field_out, all_out, left_out = refs[2 * hops : 2 * hops + 3]
    ext, low, high, scale, w0, d0, w1, d1, w2, b0, va, vb, b1, xa, xb, b2, ya, yb, kept = refs[2 * hops + 3 :]
    base = meta[0] * n - REACH
    even_group = meta[1] == 0
    own_slot = meta[2]
    lanes = table.shape[-1]
    quads = table.shape[0] // tiles
    per = SUB // R

    near = n // per
    for which, own in enumerate((panel, flags, diagonal)):
        ext[which, pl.ds(REACH // per, near)] = own[...].astype(f32)
    for k in range(1, hops + 1):
        depth = min(n, REACH - (k - 1) * n) // per
        below = (REACH - (k - 1) * n) // per - depth
        above = (REACH + k * n) // per
        for which in range(3):
            first, last = pl.ds(0, depth), pl.ds(near - depth, depth)
            ext[which, pl.ds(below, depth)] = jnp.where(even_group, mine[k - 1][which, last], theirs[k - 1][which, last])
            ext[which, pl.ds(above, depth)] = jnp.where(even_group, theirs[k - 1][which, first], mine[k - 1][which, first])

    shape = ext.shape[1:]
    position = lax.broadcasted_iota(jnp.int32, shape, 0) * per + lax.broadcasted_iota(jnp.int32, shape, 1) // R + base
    inside = (position >= 0) & (position < total)
    held = ext[1]
    coeff = ext[2] + penalty * held
    span = 1.0 + 2.0 * position.astype(f32) / total
    scale[...] = jnp.where(inside, span * (1.0 - held), 0.0).reshape(scale.shape)
    index = ext[0].astype(jnp.int32)
    low[...] = (index % lanes).reshape(low.shape)
    high[...] = (index // lanes).reshape(high.shape)
    d = coeff + 6.0
    d0[...] = d.reshape(d0.shape)
    w0[...] = jnp.where(inside, damping / d, 0.0).reshape(w0.shape)
    coeff = 0.5 * (coeff + pltpu.roll(coeff, R, 1))
    position = lax.broadcasted_iota(jnp.int32, shape, 0) + base // 2
    d = coeff + 4.5
    d1[...] = d.reshape(d1.shape)
    w1[...] = jnp.where((position >= 0) & (position < total // 2), damping / d, 0.0).reshape(w1.shape)
    coeff = coeff.reshape(shape[0] // 2, 2, *shape[1:])
    coeff = 0.5 * (coeff[:, 0] + coeff[:, 1])
    position = lax.broadcasted_iota(jnp.int32, coeff.shape, 0) + base // 4
    w2[...] = jnp.where((position >= 0) & (position < total // 4), damping / (coeff + 4.125), 0.0).reshape(w2.shape)

    def node(ref, layer, r, fine):
        return ref[pl.ds(layer * (R if fine else SUB) + r, 1), :]

    def rows(ref, layer, t):
        return [ref[layer * R + r, pl.ds(t * SUB, SUB), :] for r in range(R)]

    def put(ref, layer, t, values):
        for r in range(R):
            ref[layer * R + r, pl.ds(t * SUB, SUB), :] = values[r]

    def around(below, here, above, weight):
        out = []
        for r in range(R):
            axial = below[r] + above[r]
            if weight != 1.0:
                axial = weight * axial
            side = pltpu.roll(here[r], 1, 1) + pltpu.roll(here[r], lanes - 1, 1)
            if r > 0:
                side = side + here[r - 1]
            if r < R - 1:
                side = side + here[r + 1]
            out.append(axial + side)
        return out

    def sweep(src, dst, b, w, lo, hi, weight, fine, step=8):
        def body(layer, count):
            for t in range(tiles):
                v = [rows(src, layer + i - 1, t) for i in range(count + 2)]
                new = []
                for i in range(count):
                    nv = around(v[i], v[i + 1], v[i + 2], weight)
                    bb = rows(b, layer + i, t)
                    new.append([(1.0 - damping) * v[i + 1][r] + node(w, layer + i, r, fine) * (bb[r] + nv[r]) for r in range(R)])
                for i in range(count):
                    put(dst, layer + i, t, new[i])

        over(lo, hi, step, body)

    def loads(layer, count):
        for i in range(count):
            for r in range(R):
                lo = jnp.broadcast_to(node(low, layer + i, r, True), (SUB, lanes))
                hi = jnp.broadcast_to(node(high, layer + i, r, True), (SUB, lanes))
                factor = node(scale, layer + i, r, True)
                w = node(w0, layer + i, r, True)
                at = [hi == q for q in range(quads)]
                for t in range(tiles):
                    value = jnp.take_along_axis(table[t * quads], lo, axis=1)
                    for q in range(1, quads):
                        value = jnp.where(at[q], jnp.take_along_axis(table[t * quads + q], lo, axis=1), value)
                    value = value * factor
                    b0[(layer + i) * R + r, pl.ds(t * SUB, SUB), :] = value
                    va[(layer + i) * R + r, pl.ds(t * SUB, SUB), :] = value * w

    def residual(src, b, d, layer, t, weight, fine):
        v = [rows(src, layer + i - 1, t) for i in range(3)]
        nv = around(v[0], v[1], v[2], weight)
        bb = rows(b, layer, t)
        return [bb[r] - node(d, layer, r, fine) * v[1][r] + nv[r] for r in range(R)]

    def restrict(src, b, d, weight, fine, coarse_b, coarse_v, w, lo, hi, start, step):
        for t in range(tiles):
            put(kept, 0, t, residual(src, b, d, 2 * lo - 1, t, weight, fine))

        def body(layer, count):
            for t in range(tiles):
                before = rows(kept, 0, t)
                got = []
                for i in range(count):
                    even = residual(src, b, d, 2 * (layer + i), t, weight, fine)
                    odd = residual(src, b, d, 2 * (layer + i) + 1, t, weight, fine)
                    lead = jnp.where(layer + i + start > 0, 0.25, 0.0).astype(f32)
                    got.append([0.5 * even[r] + (0.25 * odd[r] + lead * before[r]) for r in range(R)])
                    before = odd
                put(kept, 0, t, before)
                for i in range(count):
                    put(coarse_b, layer + i, t, got[i])
                    put(coarse_v, layer + i, t, [got[i][r] * node(w, layer + i, r, False) for r in range(R)])

        over(lo, hi, step, body)

    def prolong(coarse, fine, lo, hi, start, step=4):
        def body(layer, count):
            for t in range(tiles):
                c = [rows(coarse, layer + i, t) for i in range(count + 1)]
                for i in range(count):
                    half = jnp.where(layer + i + start >= 0, 0.5, 0.0).astype(f32)
                    v = rows(fine, 2 * (layer + i), t)
                    put(fine, 2 * (layer + i), t, [v[r] + c[i][r] for r in range(R)])
                    v = rows(fine, 2 * (layer + i) + 1, t)
                    put(fine, 2 * (layer + i) + 1, t, [v[r] + half * (c[i][r] + c[i + 1][r]) for r in range(R)])

        over(lo, hi, step, body)

    first, last = REACH - BELOW, REACH + n - 1 + ABOVE
    over(first, last, 4, loads)
    sweep(va, vb, b0, w0, first + 1, last - 1, 1.0, True)
    mid, half = REACH // 2, n // 2
    restrict(vb, b0, d0, 1.0, True, b1, xa, w1, mid - 13, mid + half + 13, base // 2, 5)
    sweep(xa, xb, b1, w1, mid - 12, mid + half + 12, 0.25, False)
    low_mid, quarter = REACH // 4, n // 4
    restrict(xb, b1, d1, 0.25, False, b2, ya, w2, low_mid - 5, low_mid + quarter + 5, base // 4, 4)
    sweep(ya, yb, b2, w2, low_mid - 4, low_mid + quarter + 4, 0.0625, False)
    sweep(yb, ya, b2, w2, low_mid - 3, low_mid + quarter + 3, 0.0625, False)
    sweep(ya, yb, b2, w2, low_mid - 2, low_mid + quarter + 2, 0.0625, False)
    prolong(yb, xb, low_mid - 2, low_mid + quarter + 1, base // 4)
    sweep(xb, xa, b1, w1, mid - 3, mid + half + 2, 0.25, False)
    sweep(xa, xb, b1, w1, mid - 2, mid + half + 1, 0.25, False)
    prolong(xb, vb, mid - 2, mid + half + 1, base // 2)
    sweep(vb, va, b0, w0, REACH - 2, REACH + n + 1, 1.0, True)
    sweep(va, vb, b0, w0, REACH - 1, REACH + n, 1.0, True)

    def finish(layer, count):
        for i in range(count):
            for r in range(R):
                all_out[(layer + i - REACH) * R + r] = vb[(layer + i) * R + r]
        for t in range(own_tiles):
            tile = own_slot * own_tiles + t

            def at(ref, e, r):
                return ref[e * R + r, pl.ds(pl.multiple_of(tile * SUB, SUB), SUB), :]

            v = [[at(vb, layer + i - 1, r) for r in range(R)] for i in range(count + 2)]
            for i in range(count):
                nv = around(v[i], v[i + 1], v[i + 2], 1.0)
                for r in range(R):
                    row = (layer + i - REACH) * R + r
                    field_out[pl.ds(t * SUB, SUB), row, :] = v[i + 1][r]
                    left_out[row, pl.ds(t * SUB, SUB), :] = node(d0, layer + i, r, True) * v[i + 1][r] - nv[r]
                    left_out[row, pl.ds((own_tiles + t) * SUB, SUB), :] = at(b0, layer + i, r)

    over(REACH, REACH + n - 1, 4, finish)


def cycle(meta, table, panel, flags, diagonal, mine, theirs, cases, own, n, total, R):
    hops = len(mine)
    extent = n + 2 * REACH
    lanes = table.shape[2]

    def field(layers):
        return pltpu.VMEM((layers * R, cases, lanes), f32)

    def coefficients(rows, dtype=f32):
        return pltpu.VMEM((rows, lanes), dtype)

    fine, middle, coarse = extent * R, extent // 2 * SUB, extent // 4 * SUB
    scratch = [
        pltpu.VMEM((3, fine // SUB, SUB, lanes), f32),
        coefficients(fine, jnp.int32),
        coefficients(fine, jnp.int32),
        *(coefficients(rows) for rows in (fine, fine, fine, middle, middle, coarse)),
        *(field(extent) for _ in range(3)),
        *(field(extent // 2) for _ in range(3)),
        *(field(extent // 4) for _ in range(3)),
        field(1),
    ]
    vmem = pl.BlockSpec(memory_space=pltpu.VMEM)
    return pl.pallas_call(
        functools.partial(cycle_kernel, tiles=cases // SUB, own_tiles=own // SUB, n=n, total=total, R=R, hops=hops),
        out_shape=(
            jax.ShapeDtypeStruct((own, n * R, lanes), f32),
            jax.ShapeDtypeStruct((n * R, cases, lanes), f32),
            jax.ShapeDtypeStruct((n * R, 2 * own, lanes), f32),
        ),
        in_specs=[pl.BlockSpec(memory_space=pltpu.SMEM)] + [vmem] * (4 + 2 * hops),
        out_specs=[vmem] * 3,
        scratch_shapes=scratch,
        compiler_params=pltpu.CompilerParams(vmem_limit_bytes=48 * 2**20),
    )(meta, table, panel, flags, diagonal, *mine, *theirs)


def gram_kernel(meta, left, here, there, out, *, own):
    even_group = meta[1] == 0
    rows, cases, lanes = here.shape
    slots = cases // own

    def halves(x):
        top = x.astype(bf16)
        return top, (x - top.astype(f32)).astype(bf16)

    def dot(a, b):
        return lax.dot_general(a, b, (((1,), (1,)), ((), ())), preferred_element_type=f32)

    together = 4

    def trip(i, total):
        a = jnp.concatenate([left[i * together + j] for j in range(together)], axis=1)
        h = jnp.concatenate([here[i * together + j] for j in range(together)], axis=1)
        o = jnp.concatenate([there[i * together + j] for j in range(together)], axis=1)
        even, odd = jnp.where(even_group, h, o), jnp.where(even_group, o, h)
        parts = []
        for q in range(slots):
            parts += [even[q * own : (q + 1) * own], odd[q * own : (q + 1) * own]]
        b = jnp.concatenate(parts, axis=0)
        a_top, a_rest = halves(a)
        b_top, b_rest = halves(b)
        return total + (dot(a_top, b_top) + (dot(a_top, b_rest) + dot(a_rest, b_top)))

    out[...] = lax.fori_loop(0, rows // together, trip, jnp.zeros(out.shape, f32))


def products(meta, left, here, there, own):
    vmem = pl.BlockSpec(memory_space=pltpu.VMEM)
    return pl.pallas_call(
        functools.partial(gram_kernel, own=own),
        out_shape=jax.ShapeDtypeStruct((left.shape[1], 2 * here.shape[1]), f32),
        in_specs=[pl.BlockSpec(memory_space=pltpu.SMEM)] + [vmem] * 3,
        out_specs=vmem,
        compiler_params=pltpu.CompilerParams(vmem_limit_bytes=32 * 2**20),
    )(meta, left, here, there)


def sum_over_slabs(x):
    count = lax.axis_size("slab")
    if count & (count - 1):
        return lax.psum(x, "slab")
    by = 1
    while by < count:
        x = x + lax.ppermute(x, "slab", [(i, i ^ by) for i in range(count)])
        by *= 2
    return x


def local(pressure, panel, flags, diagonal):
    n, R, lanes = panel.shape
    slabs, groups = lax.axis_size("slab"), lax.axis_size("case")
    own = pressure.shape[0] // groups
    slots = groups // 2
    cases = own * slots
    total = n * slabs
    slab, group = lax.axis_index("slab"), lax.axis_index("case")
    meta = jnp.stack([slab, group % 2, group // 2]).astype(jnp.int32)

    per = SUB // R
    packed = [x.reshape(n // per, SUB, lanes) for x in (panel, flags, diagonal)]
    block = jnp.stack([x.astype(f32) for x in packed])
    hops = -(-REACH // n)
    mine = []
    for k in range(1, hops + 1):
        pairs = []
        for s in range(slabs):
            for g in range(groups):
                source = (s - k if g % 2 == 0 else s + k) % slabs
                pairs.append((source * groups + g, s * groups + g))
        mine.append(lax.ppermute(block, ("slab", "case"), pairs))
    swap = [(g, g ^ 1) for g in range(groups)]
    theirs = [lax.ppermute(x, "case", swap) for x in mine]

    table = pressure.reshape(slots, 2, own // SUB, SUB, -1, lanes)
    table = lax.dynamic_index_in_dim(table, group % 2, 1, keepdims=False)
    table = table.swapaxes(2, 3).reshape(-1, SUB, lanes)

    fields, worked, left = cycle(meta, table, *packed, mine, theirs, cases, own, n, total, R)
    received = lax.ppermute(worked, "case", swap)
    sums = sum_over_slabs(products(meta, left, worked, received, own))
    sums = sums * (1.0 / (total * R * lanes))
    return fields.reshape(own, n, R, lanes), sums[:own], sums[own:]


def solution(mesh):
    in_specs = (P(), P("slab", None, None), P("slab", None, None), P("slab", None, None))
    out_specs = (P("case", "slab", None, None), P("case", None), P("case", None))
    return jax.shard_map(local, mesh=mesh, in_specs=in_specs, out_specs=out_specs, check_vma=False)
```

```python
import functools

import jax
import jax.numpy as jnp
from jax import lax
from jax.experimental import pallas as pl
from jax.experimental.pallas import tpu as pltpu
from jax.sharding import PartitionSpec as P

damping = 0.7
penalty = 4.0
f32 = jnp.float32
bf16 = jnp.bfloat16
SUB = 8
REACH = 32
BELOW, ABOVE = 29, 30


def over(lo, hi, step, body):
    count = hi - lo + 1
    whole = count // step
    if whole > 1:

        def trip(i, carry):
            body(lo + i * step, step)
            return carry

        lax.fori_loop(0, whole, trip, 0)
    elif whole == 1:
        body(lo, step)
    if count - whole * step:
        body(lo + whole * step, count - whole * step)


def cycle_kernel(
    meta, table, panel, flags, diagonal, *refs, tiles, own_tiles, n, total, R, hops
):
    mine, theirs = refs[:hops], refs[hops : 2 * hops]
    field_out, all_out, left_out = refs[2 * hops : 2 * hops + 3]
    ext, low, high, scale, w0, d0, w1, d1, w2, b0, va, vb, b1, xa, xb, b2, ya, yb, kept, ring = refs[2 * hops + 3 :]
    base = meta[0] * n - REACH
    even_group = meta[1] == 0
    own_slot = meta[2]
    lanes = table.shape[-1]
    quads = table.shape[0] // tiles
    per = SUB // R

    near = n // per
    for which, own in enumerate((panel, flags, diagonal)):
        ext[which, pl.ds(REACH // per, near)] = own[...].astype(f32)
    for k in range(1, hops + 1):
        depth = min(n, REACH - (k - 1) * n) // per
        below = (REACH - (k - 1) * n) // per - depth
        above = (REACH + k * n) // per
        for which in range(3):
            first, last = pl.ds(0, depth), pl.ds(near - depth, depth)
            ext[which, pl.ds(below, depth)] = jnp.where(even_group, mine[k - 1][which, last], theirs[k - 1][which, last])
            ext[which, pl.ds(above, depth)] = jnp.where(even_group, theirs[k - 1][which, first], mine[k - 1][which, first])

    shape = ext.shape[1:]
    position = lax.broadcasted_iota(jnp.int32, shape, 0) * per + lax.broadcasted_iota(jnp.int32, shape, 1) // R + base
    inside = (position >= 0) & (position < total)
    held = ext[1]
    coeff = ext[2] + penalty * held
    span = 1.0 + 2.0 * position.astype(f32) / total
    scale[...] = jnp.where(inside, span * (1.0 - held), 0.0).reshape(scale.shape)
    index = ext[0].astype(jnp.int32)
    low[...] = (index % lanes).reshape(low.shape)
    high[...] = (index // lanes).reshape(high.shape)
    d = coeff + 6.0
    d0[...] = d.reshape(d0.shape)
    w0[...] = jnp.where(inside, damping / d, 0.0).reshape(w0.shape)
    coeff = 0.5 * (coeff + pltpu.roll(coeff, R, 1))
    position = lax.broadcasted_iota(jnp.int32, shape, 0) + base // 2
    d = coeff + 4.5
    d1[...] = d.reshape(d1.shape)
    w1[...] = jnp.where((position >= 0) & (position < total // 2), damping / d, 0.0).reshape(w1.shape)
    coeff = coeff.reshape(shape[0] // 2, 2, *shape[1:])
    coeff = 0.5 * (coeff[:, 0] + coeff[:, 1])
    position = lax.broadcasted_iota(jnp.int32, coeff.shape, 0) + base // 4
    w2[...] = jnp.where((position >= 0) & (position < total // 4), damping / (coeff + 4.125), 0.0).reshape(w2.shape)

    def node(ref, layer, r, fine):
        return ref[pl.ds(layer * (R if fine else SUB) + r, 1), :]

    def rows(ref, layer, t):
        return [ref[layer * R + r, pl.ds(t * SUB, SUB), :] for r in range(R)]

    def put(ref, layer, t, values):
        for r in range(R):
            ref[layer * R + r, pl.ds(t * SUB, SUB), :] = values[r]

    cases = tiles * SUB
    to = lax.broadcasted_iota(jnp.int32, (lanes, lanes), 0)
    fro = lax.broadcasted_iota(jnp.int32, (lanes, lanes), 1)
    step_apart = ((to - fro) % lanes == 1) | ((fro - to) % lanes == 1)
    ring[...] = jnp.where(step_apart, 1.0, 0.0).astype(bf16)

    def beside(x):
        flat = x.reshape(-1, lanes)
        top = flat.astype(bf16)
        rest = (flat - top.astype(f32)).astype(bf16)
        both = jnp.concatenate([top, rest], axis=1)
        two = jnp.concatenate([ring[...], ring[...]], axis=0)
        return jnp.dot(both, two, preferred_element_type=f32).reshape(x.shape)

    def block(ref, layer, count):
        return ref[pl.ds(layer * R, count * R)]

    def neighbours(src, layer, count, weight):
        by_matrix = [(i, r) for i in range(count) for r in range(R) if r % 2 == 0]
        flat = [src[(layer + i) * R + r] for i, r in by_matrix]
        got = beside(jnp.concatenate(flat, axis=0))
        side = {key: got[j * cases : (j + 1) * cases] for j, key in enumerate(by_matrix)}
        out = []
        for i in range(count):
            line = []
            for r in range(R):
                axial = src[(layer + i - 1) * R + r] + src[(layer + i + 1) * R + r]
                if weight != 1.0:
                    axial = weight * axial
                if (i, r) in side:
                    beside_it = side[i, r]
                else:
                    here = src[(layer + i) * R + r]
                    beside_it = jnp.concatenate([pltpu.roll(here[q * SUB : (q + 1) * SUB], 1, 1) + pltpu.roll(here[q * SUB : (q + 1) * SUB], lanes - 1, 1) for q in range(tiles)], axis=0)
                x = axial + beside_it
                if r > 0:
                    x = x + src[(layer + i) * R + r - 1]
                if r < R - 1:
                    x = x + src[(layer + i) * R + r + 1]
                line.append(x)
            out.append(line)
        return out

    def sweep(src, dst, b, w, lo, hi, weight, fine, step=8):
        def body(layer, count):
            nv = neighbours(src, layer, count, weight)
            for i in range(count):
                for r in range(R):
                    row = (layer + i) * R + r
                    dst[row] = (1.0 - damping) * src[row] + node(w, layer + i, r, fine) * (b[row] + nv[i][r])

        over(lo, hi, step, body)

    def loads(layer, count):
        for i in range(count):
            for r in range(R):
                lo = jnp.broadcast_to(node(low, layer + i, r, True), (SUB, lanes))
                hi = jnp.broadcast_to(node(high, layer + i, r, True), (SUB, lanes))
                factor = node(scale, layer + i, r, True)
                w = node(w0, layer + i, r, True)
                at = [hi == q for q in range(quads)]
                for t in range(tiles):
                    value = jnp.take_along_axis(table[t * quads], lo, axis=1)
                    for q in range(1, quads):
                        value = jnp.where(at[q], jnp.take_along_axis(table[t * quads + q], lo, axis=1), value)
                    value = value * factor
                    b0[(layer + i) * R + r, pl.ds(t * SUB, SUB), :] = value
                    va[(layer + i) * R + r, pl.ds(t * SUB, SUB), :] = value * w

    def residual(src, b, d, layer, count, weight, fine):
        nv = neighbours(src, layer, count, weight)
        return [[b[(layer + i) * R + r] - node(d, layer + i, r, fine) * src[(layer + i) * R + r] + nv[i][r]
                 for r in range(R)] for i in range(count)]

    def restrict(src, b, d, weight, fine, coarse_b, coarse_v, w, lo, hi, start, step):
        first = residual(src, b, d, 2 * lo - 1, 1, weight, fine)[0]
        for r in range(R):
            kept[r] = first[r]

        def body(layer, count):
            f = residual(src, b, d, 2 * layer, 2 * count, weight, fine)
            for i in range(count):
                lead = jnp.where(layer + i + start > 0, 0.25, 0.0).astype(f32)
                for r in range(R):
                    before = kept[r] if i == 0 else f[2 * i - 1][r]
                    value = 0.5 * f[2 * i][r] + (0.25 * f[2 * i + 1][r] + lead * before)
                    row = (layer + i) * R + r
                    coarse_b[row] = value
                    coarse_v[row] = value * node(w, layer + i, r, False)
            for r in range(R):
                kept[r] = f[-1][r]

        over(lo, hi, step, body)

    def prolong(coarse, fine, lo, hi, start, step=4):
        def body(layer, count):
            for t in range(tiles):
                c = [rows(coarse, layer + i, t) for i in range(count + 1)]
                for i in range(count):
                    half = jnp.where(layer + i + start >= 0, 0.5, 0.0).astype(f32)
                    v = rows(fine, 2 * (layer + i), t)
                    put(fine, 2 * (layer + i), t, [v[r] + c[i][r] for r in range(R)])
                    v = rows(fine, 2 * (layer + i) + 1, t)
                    put(fine, 2 * (layer + i) + 1, t, [v[r] + half * (c[i][r] + c[i + 1][r]) for r in range(R)])

        over(lo, hi, step, body)

    first, last = REACH - BELOW, REACH + n - 1 + ABOVE
    over(first, last, 18, loads)
    sweep(va, vb, b0, w0, first + 1, last - 1, 1.0, True, 23)
    mid, half = REACH // 2, n // 2
    restrict(vb, b0, d0, 1.0, True, b1, xa, w1, mid - 13, mid + half + 13, base // 2, 11)
    sweep(xa, xb, b1, w1, mid - 12, mid + half + 12, 0.25, False, 16)
    low_mid, quarter = REACH // 4, n // 4
    restrict(xb, b1, d1, 0.25, False, b2, ya, w2, low_mid - 5, low_mid + quarter + 5, base // 4, 7)
    sweep(ya, yb, b2, w2, low_mid - 4, low_mid + quarter + 4, 0.0625, False, 6)
    sweep(yb, ya, b2, w2, low_mid - 3, low_mid + quarter + 3, 0.0625, False, 6)
    sweep(ya, yb, b2, w2, low_mid - 2, low_mid + quarter + 2, 0.0625, False, 6)
    prolong(yb, xb, low_mid - 2, low_mid + quarter + 1, base // 4, 7)
    sweep(xb, xa, b1, w1, mid - 3, mid + half + 2, 0.25, False, 12)
    sweep(xa, xb, b1, w1, mid - 2, mid + half + 1, 0.25, False, 12)
    prolong(xb, vb, mid - 2, mid + half + 1, base // 2, 9)
    sweep(vb, va, b0, w0, REACH - 2, REACH + n + 1, 1.0, True, 16)
    sweep(va, vb, b0, w0, REACH - 1, REACH + n, 1.0, True, 16)

    own = own_tiles * SUB

    def finish(layer, count):
        nv = neighbours(vb, layer, count, 1.0)
        for i in range(count):
            for r in range(R):
                at = (layer + i) * R + r
                row = (layer + i - REACH) * R + r
                here = vb[at]
                all_out[row] = here
                image = node(d0, layer + i, r, True) * here - nv[i][r]
                load = b0[at]
                def mine_of(x):
                    return jnp.where(own_slot == 0, x[:own], x[own:])
                field_out[:, row, :] = mine_of(here)
                left_out[row, pl.ds(0, own), :] = mine_of(image)
                left_out[row, pl.ds(own, own), :] = mine_of(load)

    over(REACH, REACH + n - 1, 12, finish)


def cycle(meta, table, panel, flags, diagonal, mine, theirs, cases, own, n, total, R):
    hops = len(mine)
    extent = n + 2 * REACH
    lanes = table.shape[2]

    def field(layers):
        return pltpu.VMEM((layers * R, cases, lanes), f32)

    def coefficients(rows, dtype=f32):
        return pltpu.VMEM((rows, lanes), dtype)

    fine, middle, coarse = extent * R, extent // 2 * SUB, extent // 4 * SUB
    scratch = [
        pltpu.VMEM((3, fine // SUB, SUB, lanes), f32),
        coefficients(fine, jnp.int32),
        coefficients(fine, jnp.int32),
        *(coefficients(rows) for rows in (fine, fine, fine, middle, middle, coarse)),
        *(field(extent) for _ in range(3)),
        *(field(extent // 2) for _ in range(3)),
        *(field(extent // 4) for _ in range(3)),
        field(1),
        pltpu.VMEM((lanes, lanes), bf16),
    ]
    vmem = pl.BlockSpec(memory_space=pltpu.VMEM)
    return pl.pallas_call(
        functools.partial(cycle_kernel, tiles=cases // SUB, own_tiles=own // SUB, n=n, total=total, R=R, hops=hops),
        out_shape=(
            jax.ShapeDtypeStruct((own, n * R, lanes), f32),
            jax.ShapeDtypeStruct((n * R, cases, lanes), f32),
            jax.ShapeDtypeStruct((n * R, 2 * own, lanes), f32),
        ),
        in_specs=[pl.BlockSpec(memory_space=pltpu.SMEM)] + [vmem] * (4 + 2 * hops),
        out_specs=[vmem] * 3,
        scratch_shapes=scratch,
        compiler_params=pltpu.CompilerParams(vmem_limit_bytes=48 * 2**20),
    )(meta, table, panel, flags, diagonal, *mine, *theirs)


def halves(x):
    top = x.astype(bf16)
    return top, (x - top.astype(f32)).astype(bf16)


def partial_products(left, right, together=12):
    rows = right.shape[0]
    total = 0.0
    for i in range(0, rows, together):
        a = jnp.concatenate([left[i + j] for j in range(together)], axis=1)
        b = jnp.concatenate([right[i + j] for j in range(together)], axis=1)
        a_top, a_rest = halves(a)
        b_top, b_rest = halves(b)

        def dot(x, y):
            return lax.dot_general(x, y, (((1,), (1,)), ((), ())), preferred_element_type=f32)

        both = dot(jnp.concatenate([a_top, a_rest], axis=0), b_top)
        total = total + (both[: a.shape[0]] + (both[a.shape[0] :] + dot(a_top, b_rest)))
    return total


def near_kernel(left, here, out):
    out[...] = partial_products(left, here)


def far_kernel(meta, left, there, near, out, *, own):
    here, other = near[...], partial_products(left, there)
    even_group = meta[1] == 0
    even, odd = jnp.where(even_group, here, other), jnp.where(even_group, other, here)
    parts = []
    for q in range(here.shape[1] // own):
        parts += [even[:, q * own : (q + 1) * own], odd[:, q * own : (q + 1) * own]]
    out[...] = jnp.concatenate(parts, axis=1)


def near_products(left, here):
    rows, m, lanes = left.shape
    cases = here.shape[1]
    vmem = pl.BlockSpec(memory_space=pltpu.VMEM)
    return pl.pallas_call(
        near_kernel,
        out_shape=jax.ShapeDtypeStruct((m, cases), f32),
        in_specs=[vmem] * 2,
        out_specs=vmem,
        cost_estimate=pl.CostEstimate(flops=6 * rows * m * cases * lanes, bytes_accessed=4 * rows * (m + cases) * lanes, transcendentals=0),
        compiler_params=pltpu.CompilerParams(vmem_limit_bytes=32 * 2**20),
    )(left, here)


def far_products(meta, left, there, near, own):
    vmem = pl.BlockSpec(memory_space=pltpu.VMEM)
    return pl.pallas_call(
        functools.partial(far_kernel, own=own),
        out_shape=jax.ShapeDtypeStruct((near.shape[0], 2 * near.shape[1]), f32),
        in_specs=[pl.BlockSpec(memory_space=pltpu.SMEM)] + [vmem] * 3,
        out_specs=vmem,
        compiler_params=pltpu.CompilerParams(vmem_limit_bytes=32 * 2**20),
    )(meta, left, there, near)


def sum_over_slabs(x):
    count = lax.axis_size("slab")
    if count & (count - 1):
        return lax.psum(x, "slab")
    by = 1
    while by < count:
        x = x + lax.ppermute(x, "slab", [(i, i ^ by) for i in range(count)])
        by *= 2
    return x


def local(pressure, panel, flags, diagonal):
    n, R, lanes = panel.shape
    slabs, groups = lax.axis_size("slab"), lax.axis_size("case")
    own = pressure.shape[0] // groups
    slots = groups // 2
    cases = own * slots
    total = n * slabs
    slab, group = lax.axis_index("slab"), lax.axis_index("case")
    meta = jnp.stack([slab, group % 2, group // 2]).astype(jnp.int32)

    per = SUB // R
    packed = [x.reshape(n // per, SUB, lanes) for x in (panel, flags, diagonal)]
    block = jnp.stack([x.astype(f32) for x in packed])
    hops = -(-REACH // n)
    mine = []
    for k in range(1, hops + 1):
        pairs = []
        for s in range(slabs):
            for g in range(groups):
                to = s + k if g % 2 == 0 else s - k
                pairs.append((s * groups + g, to * groups + g if 0 <= to < slabs else s * groups + (g ^ 1)))
        mine.append(lax.ppermute(block, ("slab", "case"), pairs))
    swap = [(g, g ^ 1) for g in range(groups)]
    theirs = [lax.ppermute(x, "case", swap) for x in mine]

    table = pressure.reshape(slots, 2, own // SUB, SUB, -1, lanes)
    table = lax.dynamic_index_in_dim(table, group % 2, 1, keepdims=False)
    table = table.swapaxes(2, 3).reshape(-1, SUB, lanes)

    fields, worked, left = cycle(meta, table, *packed, mine, theirs, cases, own, n, total, R)
    received = lax.ppermute(worked, "case", swap)
    near = near_products(left, worked)
    sums = sum_over_slabs(far_products(meta, left, received, near, own))
    sums = sums * (1.0 / (total * R * lanes))
    return fields.reshape(own, n, R, lanes), sums[:own], sums[own:]


def solution(mesh):
    in_specs = (P(), P("slab", None, None), P("slab", None, None), P("slab", None, None))
    out_specs = (P("case", "slab", None, None), P("case", None), P("case", None))
    return jax.shard_map(local, mesh=mesh, in_specs=in_specs, out_specs=out_specs, check_vma=False)
```

```python
import functools

import jax
import jax.numpy as jnp
from jax import lax
from jax.experimental import pallas as pl
from jax.experimental.pallas import tpu as pltpu
from jax.sharding import PartitionSpec as P

damping = 0.7
penalty = 4.0
f32 = jnp.float32
bf16 = jnp.bfloat16
SUB = 8
REACH = 32
BELOW, ABOVE = 29, 30


def over(lo, hi, step, body):
    count = hi - lo + 1
    whole = count // step
    if whole > 1:

        def trip(i, carry):
            body(lo + i * step, step)
            return carry

        lax.fori_loop(0, whole, trip, 0)
    elif whole == 1:
        body(lo, step)
    if count - whole * step:
        body(lo + whole * step, count - whole * step)


def cycle_kernel(
    meta, table, panel, flags, diagonal, *refs, tiles, own_tiles, n, total, R, hops
):
    mine, theirs = refs[:hops], refs[hops : 2 * hops]
    field_out, all_out, left_out = refs[2 * hops : 2 * hops + 3]
    ext, picked, scale, w0, d0, w1, d1, w2, b0, va, vb, b1, xa, xb, b2, ya, yb, kept, ring, stack = refs[2 * hops + 3 :]
    base = meta[0] * n - REACH
    even_group = meta[1] == 0
    own_slot = meta[2]
    lanes = table.shape[-1]
    quads = table.shape[0] // tiles
    per = SUB // R

    near = n // per
    for which, own in enumerate((panel, flags, diagonal)):
        ext[which, pl.ds(REACH // per, near)] = own[...].astype(f32)
    for k in range(1, hops + 1):
        depth = min(n, REACH - (k - 1) * n) // per
        below = (REACH - (k - 1) * n) // per - depth
        above = (REACH + k * n) // per
        for which in range(3):
            first, last = pl.ds(0, depth), pl.ds(near - depth, depth)
            ext[which, pl.ds(below, depth)] = jnp.where(even_group, mine[k - 1][which, last], theirs[k - 1][which, last])
            ext[which, pl.ds(above, depth)] = jnp.where(even_group, theirs[k - 1][which, first], mine[k - 1][which, first])

    shape = ext.shape[1:]
    position = lax.broadcasted_iota(jnp.int32, shape, 0) * per + lax.broadcasted_iota(jnp.int32, shape, 1) // R + base
    inside = (position >= 0) & (position < total)
    held = ext[1]
    coeff = ext[2] + penalty * held
    span = 1.0 + 2.0 * position.astype(f32) / total
    scale[...] = jnp.where(inside, span * (1.0 - held), 0.0).reshape(scale.shape)
    index = ext[0].astype(jnp.int32)
    picked[...] = index.reshape(picked.shape)
    d = coeff + 6.0
    d0[...] = d.reshape(d0.shape)
    w0[...] = jnp.where(inside, damping / d, 0.0).reshape(w0.shape)
    coeff = 0.5 * (coeff + pltpu.roll(coeff, R, 1))
    position = lax.broadcasted_iota(jnp.int32, shape, 0) + base // 2
    d = coeff + 4.5
    d1[...] = d.reshape(d1.shape)
    w1[...] = jnp.where((position >= 0) & (position < total // 2), damping / d, 0.0).reshape(w1.shape)
    coeff = coeff.reshape(shape[0] // 2, 2, *shape[1:])
    coeff = 0.5 * (coeff[:, 0] + coeff[:, 1])
    position = lax.broadcasted_iota(jnp.int32, coeff.shape, 0) + base // 4
    w2[...] = jnp.where((position >= 0) & (position < total // 4), damping / (coeff + 4.125), 0.0).reshape(w2.shape)

    def node(ref, layer, r, fine):
        return ref[pl.ds(layer * (R if fine else SUB) + r, 1), :]

    def rows(ref, layer, t):
        return [ref[layer * R + r, pl.ds(t * SUB, SUB), :] for r in range(R)]

    def put(ref, layer, t, values):
        for r in range(R):
            ref[layer * R + r, pl.ds(t * SUB, SUB), :] = values[r]

    cases = tiles * SUB
    to = lax.broadcasted_iota(jnp.int32, (lanes, lanes), 0)
    fro = lax.broadcasted_iota(jnp.int32, (lanes, lanes), 1)
    step_apart = ((to - fro) % lanes == 1) | ((fro - to) % lanes == 1)
    ring[...] = jnp.where(step_apart, 1.0, 0.0).astype(bf16)

    def beside(x):
        flat = x.reshape(-1, lanes)
        top = flat.astype(bf16)
        rest = (flat - top.astype(f32)).astype(bf16)
        both = jnp.concatenate([top, rest], axis=1)
        two = jnp.concatenate([ring[...], ring[...]], axis=0)
        return jnp.dot(both, two, preferred_element_type=f32).reshape(x.shape)

    def block(ref, layer, count):
        return ref[pl.ds(layer * R, count * R)]

    def neighbours(src, layer, count, weight):
        by_matrix = [(i, r) for i in range(count) for r in range(R) if r % 2 == 0]
        flat = [src[(layer + i) * R + r] for i, r in by_matrix]
        got = beside(jnp.concatenate(flat, axis=0))
        side = {key: got[j * cases : (j + 1) * cases] for j, key in enumerate(by_matrix)}
        out = []
        for i in range(count):
            line = []
            for r in range(R):
                axial = src[(layer + i - 1) * R + r] + src[(layer + i + 1) * R + r]
                if weight != 1.0:
                    axial = weight * axial
                if (i, r) in side:
                    beside_it = side[i, r]
                else:
                    here = src[(layer + i) * R + r]
                    beside_it = jnp.concatenate([pltpu.roll(here[q * SUB : (q + 1) * SUB], 1, 1) + pltpu.roll(here[q * SUB : (q + 1) * SUB], lanes - 1, 1) for q in range(tiles)], axis=0)
                x = axial + beside_it
                if r > 0:
                    x = x + src[(layer + i) * R + r - 1]
                if r < R - 1:
                    x = x + src[(layer + i) * R + r + 1]
                line.append(x)
            out.append(line)
        return out

    def sweep(src, dst, b, w, lo, hi, weight, fine, step=8):
        def body(layer, count):
            nv = neighbours(src, layer, count, weight)
            for i in range(count):
                for r in range(R):
                    row = (layer + i) * R + r
                    dst[row] = (1.0 - damping) * src[row] + node(w, layer + i, r, fine) * (b[row] + nv[i][r])

        over(lo, hi, step, body)

    pair = 2 * lanes
    wide = quads // 2
    for h in range(wide):
        both = jnp.concatenate([jnp.concatenate([table[t * quads + 2 * h], table[t * quads + 2 * h + 1]], axis=1) for t in range(tiles)], axis=0)
        top = both.astype(bf16)
        stack[pl.ds(2 * h * cases, cases), :] = top
        stack[pl.ds((2 * h + 1) * cases, cases), :] = (both - top.astype(f32)).astype(bf16)

    def by_matrix(index):
        spot = lax.broadcasted_iota(jnp.int16, (pair, lanes), 0)
        place = jnp.broadcast_to(index & (pair - 1), (2 * SUB, lanes)).astype(jnp.int16)
        place = jnp.concatenate([place] * (pair // (2 * SUB)), axis=0)
        hot = jnp.where(spot == place, jnp.ones((), bf16), jnp.zeros((), bf16))
        got = jnp.dot(stack[...], hot, preferred_element_type=f32)
        value = got[:cases] + got[cases : 2 * cases]
        for h in range(1, wide):
            value = jnp.where(jnp.broadcast_to(index, value.shape) >= h * pair, got[2 * h * cases : (2 * h + 1) * cases] + got[(2 * h + 1) * cases : (2 * h + 2) * cases], value)
        return value

    def by_lanes(index):
        wide_index = jnp.broadcast_to(index, (SUB, lanes))
        low = jnp.broadcast_to(index & (lanes - 1), (SUB, lanes))
        beyond = [wide_index >= q * lanes for q in range(1, quads)]
        out = []
        for t in range(tiles):
            value = jnp.take_along_axis(table[t * quads], low, axis=1)
            for q in range(1, quads):
                value = jnp.where(beyond[q - 1], jnp.take_along_axis(table[t * quads + q], low, axis=1), value)
            out.append(value)
        return jnp.concatenate(out, axis=0)

    def loads(layer, count):
        for i in range(count):
            for r in range(R):
                index = node(picked, layer + i, r, True)
                value = by_matrix(index) if r % 2 else by_lanes(index)
                value = value * node(scale, layer + i, r, True)
                b0[(layer + i) * R + r] = value
                va[(layer + i) * R + r] = value * node(w0, layer + i, r, True)

    def residual(src, b, d, layer, count, weight, fine):
        nv = neighbours(src, layer, count, weight)
        return [[b[(layer + i) * R + r] - node(d, layer + i, r, fine) * src[(layer + i) * R + r] + nv[i][r]
                 for r in range(R)] for i in range(count)]

    def restrict(src, b, d, weight, fine, coarse_b, coarse_v, w, lo, hi, start, step):
        first = residual(src, b, d, 2 * lo - 1, 1, weight, fine)[0]
        for r in range(R):
            kept[r] = first[r]

        def body(layer, count):
            f = residual(src, b, d, 2 * layer, 2 * count, weight, fine)
            for i in range(count):
                lead = jnp.where(layer + i + start > 0, 0.25, 0.0).astype(f32)
                for r in range(R):
                    before = kept[r] if i == 0 else f[2 * i - 1][r]
                    value = 0.5 * f[2 * i][r] + (0.25 * f[2 * i + 1][r] + lead * before)
                    row = (layer + i) * R + r
                    coarse_b[row] = value
                    coarse_v[row] = value * node(w, layer + i, r, False)
            for r in range(R):
                kept[r] = f[-1][r]

        over(lo, hi, step, body)

    def prolong(coarse, fine, lo, hi, start, step=4):
        def body(layer, count):
            for t in range(tiles):
                c = [rows(coarse, layer + i, t) for i in range(count + 1)]
                for i in range(count):
                    half = jnp.where(layer + i + start >= 0, 0.5, 0.0).astype(f32)
                    v = rows(fine, 2 * (layer + i), t)
                    put(fine, 2 * (layer + i), t, [v[r] + c[i][r] for r in range(R)])
                    v = rows(fine, 2 * (layer + i) + 1, t)
                    put(fine, 2 * (layer + i) + 1, t, [v[r] + half * (c[i][r] + c[i + 1][r]) for r in range(R)])

        over(lo, hi, step, body)

    first, last = REACH - BELOW, REACH + n - 1 + ABOVE
    over(first, last, 18, loads)
    sweep(va, vb, b0, w0, first + 1, last - 1, 1.0, True, 23)
    mid, half = REACH // 2, n // 2
    restrict(vb, b0, d0, 1.0, True, b1, xa, w1, mid - 13, mid + half + 13, base // 2, 11)
    sweep(xa, xb, b1, w1, mid - 12, mid + half + 12, 0.25, False, 16)
    low_mid, quarter = REACH // 4, n // 4
    restrict(xb, b1, d1, 0.25, False, b2, ya, w2, low_mid - 5, low_mid + quarter + 5, base // 4, 14)
    sweep(ya, yb, b2, w2, low_mid - 4, low_mid + quarter + 4, 0.0625, False, 12)
    sweep(yb, ya, b2, w2, low_mid - 3, low_mid + quarter + 3, 0.0625, False, 12)
    sweep(ya, yb, b2, w2, low_mid - 2, low_mid + quarter + 2, 0.0625, False, 12)
    prolong(yb, xb, low_mid - 2, low_mid + quarter + 1, base // 4, 7)
    sweep(xb, xa, b1, w1, mid - 3, mid + half + 2, 0.25, False, 12)
    sweep(xa, xb, b1, w1, mid - 2, mid + half + 1, 0.25, False, 12)
    prolong(xb, vb, mid - 2, mid + half + 1, base // 2, 9)
    sweep(vb, va, b0, w0, REACH - 2, REACH + n + 1, 1.0, True, 16)
    sweep(va, vb, b0, w0, REACH - 1, REACH + n, 1.0, True, 16)

    own = own_tiles * SUB

    def finish(layer, count):
        nv = neighbours(vb, layer, count, 1.0)
        for i in range(count):
            for r in range(R):
                at = (layer + i) * R + r
                row = (layer + i - REACH) * R + r
                here = vb[at]
                all_out[row] = here
                image = node(d0, layer + i, r, True) * here - nv[i][r]
                load = b0[at]
                def mine_of(x):
                    return jnp.where(own_slot == 0, x[:own], x[own:])
                field_out[:, row, :] = mine_of(here)
                left_out[row, pl.ds(0, own), :] = mine_of(image)
                left_out[row, pl.ds(own, own), :] = mine_of(load)

    over(REACH, REACH + n - 1, 12, finish)


def cycle(meta, table, panel, flags, diagonal, mine, theirs, cases, own, n, total, R):
    hops = len(mine)
    extent = n + 2 * REACH
    lanes = table.shape[2]

    def field(layers):
        return pltpu.VMEM((layers * R, cases, lanes), f32)

    def coefficients(rows, dtype=f32):
        return pltpu.VMEM((rows, lanes), dtype)

    fine, middle, coarse = extent * R, extent // 2 * SUB, extent // 4 * SUB
    scratch = [
        pltpu.VMEM((3, fine // SUB, SUB, lanes), f32),
        coefficients(fine, jnp.int32),
        *(coefficients(rows) for rows in (fine, fine, fine, middle, middle, coarse)),
        *(field(extent) for _ in range(3)),
        *(field(extent // 2) for _ in range(3)),
        *(field(extent // 4) for _ in range(3)),
        field(1),
        pltpu.VMEM((lanes, lanes), bf16),
        pltpu.VMEM((cases * table.shape[0] * SUB // cases, 2 * lanes), bf16),
    ]
    vmem = pl.BlockSpec(memory_space=pltpu.VMEM)
    return pl.pallas_call(
        functools.partial(cycle_kernel, tiles=cases // SUB, own_tiles=own // SUB, n=n, total=total, R=R, hops=hops),
        out_shape=(
            jax.ShapeDtypeStruct((own, n * R, lanes), f32),
            jax.ShapeDtypeStruct((n * R, cases, lanes), f32),
            jax.ShapeDtypeStruct((n * R, 2 * own, lanes), f32),
        ),
        in_specs=[pl.BlockSpec(memory_space=pltpu.SMEM)] + [vmem] * (4 + 2 * hops),
        out_specs=[vmem] * 3,
        scratch_shapes=scratch,
        compiler_params=pltpu.CompilerParams(vmem_limit_bytes=48 * 2**20),
    )(meta, table, panel, flags, diagonal, *mine, *theirs)


def halves(x):
    top = x.astype(bf16)
    return top, (x - top.astype(f32)).astype(bf16)


def partial_products(left, right, together=12):
    rows = right.shape[0]
    total = 0.0
    for i in range(0, rows, together):
        a = jnp.concatenate([left[i + j] for j in range(together)], axis=1)
        b = jnp.concatenate([right[i + j] for j in range(together)], axis=1)
        a_top, a_rest = halves(a)
        b_top, b_rest = halves(b)

        def dot(x, y):
            return lax.dot_general(x, y, (((1,), (1,)), ((), ())), preferred_element_type=f32)

        both = dot(jnp.concatenate([a_top, a_rest], axis=0), b_top)
        total = total + (both[: a.shape[0]] + (both[a.shape[0] :] + dot(a_top, b_rest)))
    return total


def near_kernel(left, here, out):
    out[...] = partial_products(left, here)


def far_kernel(meta, left, there, near, out, *, own):
    here, other = near[...], partial_products(left, there)
    even_group = meta[1] == 0
    even, odd = jnp.where(even_group, here, other), jnp.where(even_group, other, here)
    parts = []
    for q in range(here.shape[1] // own):
        parts += [even[:, q * own : (q + 1) * own], odd[:, q * own : (q + 1) * own]]
    out[...] = jnp.concatenate(parts, axis=1)


def near_products(left, here):
    rows, m, lanes = left.shape
    cases = here.shape[1]
    vmem = pl.BlockSpec(memory_space=pltpu.VMEM)
    return pl.pallas_call(
        near_kernel,
        out_shape=jax.ShapeDtypeStruct((m, cases), f32),
        in_specs=[vmem] * 2,
        out_specs=vmem,
        cost_estimate=pl.CostEstimate(flops=6 * rows * m * cases * lanes, bytes_accessed=4 * rows * (m + cases) * lanes, transcendentals=0),
        compiler_params=pltpu.CompilerParams(vmem_limit_bytes=32 * 2**20),
    )(left, here)


def far_products(meta, left, there, near, own):
    vmem = pl.BlockSpec(memory_space=pltpu.VMEM)
    return pl.pallas_call(
        functools.partial(far_kernel, own=own),
        out_shape=jax.ShapeDtypeStruct((near.shape[0], 2 * near.shape[1]), f32),
        in_specs=[pl.BlockSpec(memory_space=pltpu.SMEM)] + [vmem] * 3,
        out_specs=vmem,
        compiler_params=pltpu.CompilerParams(vmem_limit_bytes=32 * 2**20),
    )(meta, left, there, near)


def sum_over_slabs(x):
    count = lax.axis_size("slab")
    if count & (count - 1):
        return lax.psum(x, "slab")
    by = 1
    while by < count:
        x = x + lax.ppermute(x, "slab", [(i, i ^ by) for i in range(count)])
        by *= 2
    return x


def local(pressure, panel, flags, diagonal):
    n, R, lanes = panel.shape
    slabs, groups = lax.axis_size("slab"), lax.axis_size("case")
    own = pressure.shape[0] // groups
    slots = groups // 2
    cases = own * slots
    total = n * slabs
    slab, group = lax.axis_index("slab"), lax.axis_index("case")
    meta = jnp.stack([slab, group % 2, group // 2]).astype(jnp.int32)

    per = SUB // R
    packed = [x.reshape(n // per, SUB, lanes) for x in (panel, flags, diagonal)]
    block = jnp.stack([x.astype(f32) for x in packed])
    hops = -(-REACH // n)
    mine = []
    for k in range(1, hops + 1):
        pairs = []
        for s in range(slabs):
            for g in range(groups):
                to = s + k if g % 2 == 0 else s - k
                pairs.append((s * groups + g, to * groups + g if 0 <= to < slabs else s * groups + (g ^ 1)))
        mine.append(lax.ppermute(block, ("slab", "case"), pairs))
    swap = [(g, g ^ 1) for g in range(groups)]
    theirs = [lax.ppermute(x, "case", swap) for x in mine]

    table = pressure.reshape(slots, 2, own // SUB, SUB, -1, lanes)
    table = lax.dynamic_index_in_dim(table, group % 2, 1, keepdims=False)
    table = table.swapaxes(2, 3).reshape(-1, SUB, lanes)

    fields, worked, left = cycle(meta, table, *packed, mine, theirs, cases, own, n, total, R)
    received = lax.ppermute(worked, "case", swap)
    near = near_products(left, worked)
    sums = sum_over_slabs(far_products(meta, left, received, near, own))
    sums = sums * (1.0 / (total * R * lanes))
    return fields.reshape(own, n, R, lanes), sums[:own], sums[own:]


def solution(mesh):
    in_specs = (P(), P("slab", None, None), P("slab", None, None), P("slab", None, None))
    out_specs = (P("case", "slab", None, None), P("case", None), P("case", None))
    return jax.shard_map(local, mesh=mesh, in_specs=in_specs, out_specs=out_specs, check_vma=False)
```

```python
import functools

import jax
import jax.numpy as jnp
from jax import lax
from jax.experimental import pallas as pl
from jax.experimental.pallas import tpu as pltpu
from jax.sharding import PartitionSpec as P

damping = 0.7
penalty = 4.0
f32 = jnp.float32
bf16 = jnp.bfloat16
SUB = 8
REACH = 32
BELOW, ABOVE = 29, 30


def over(lo, hi, step, body):
    count = hi - lo + 1
    whole = count // step
    if whole > 1:

        def trip(i, carry):
            body(lo + i * step, step)
            return carry

        lax.fori_loop(0, whole, trip, 0)
    elif whole == 1:
        body(lo, step)
    if count - whole * step:
        body(lo + whole * step, count - whole * step)


def cycle_kernel(
    table, block, *refs, tiles, own_tiles, n, total, R, hops
):
    mine, theirs = refs[:hops], refs[hops : 2 * hops]
    field_out, first_out, second_out, left_out = refs[2 * hops : 2 * hops + 4]
    split = first_out.shape[0]
    ext, picked, scale, w0, d0, w1, d1, w2, b0, va, vb, b1, xa, xb, b2, ya, yb, kept, ring, stack = refs[2 * hops + 4 :]
    base = lax.axis_index("slab") * n - REACH
    group = lax.axis_index("case")
    even_group = group % 2 == 0
    own_slot = group // 2
    lanes = table.shape[-1]
    quads = table.shape[0] // tiles
    per = SUB // R

    near = n // per
    for which in range(3):
        ext[which, pl.ds(REACH // per, near)] = block[which]
    for k in range(1, hops + 1):
        depth = min(n, REACH - (k - 1) * n) // per
        below = (REACH - (k - 1) * n) // per - depth
        above = (REACH + k * n) // per
        for which in range(3):
            first, last = pl.ds(0, depth), pl.ds(near - depth, depth)
            ext[which, pl.ds(below, depth)] = jnp.where(even_group, mine[k - 1][which, last], theirs[k - 1][which, last])
            ext[which, pl.ds(above, depth)] = jnp.where(even_group, theirs[k - 1][which, first], mine[k - 1][which, first])

    shape = ext.shape[1:]
    position = lax.broadcasted_iota(jnp.int32, shape, 0) * per + lax.broadcasted_iota(jnp.int32, shape, 1) // R + base
    inside = (position >= 0) & (position < total)
    held = ext[1]
    coeff = ext[2] + penalty * held
    span = 1.0 + 2.0 * position.astype(f32) / total
    scale[...] = jnp.where(inside, span * (1.0 - held), 0.0).reshape(scale.shape)
    index = ext[0].astype(jnp.int32)
    picked[...] = index.reshape(picked.shape)
    d = coeff + 6.0
    d0[...] = d.reshape(d0.shape)
    w0[...] = jnp.where(inside, damping / d, 0.0).reshape(w0.shape)
    coeff = 0.5 * (coeff + pltpu.roll(coeff, R, 1))
    position = lax.broadcasted_iota(jnp.int32, shape, 0) + base // 2
    d = coeff + 4.5
    d1[...] = d.reshape(d1.shape)
    w1[...] = jnp.where((position >= 0) & (position < total // 2), damping / d, 0.0).reshape(w1.shape)
    coeff = coeff.reshape(shape[0] // 2, 2, *shape[1:])
    coeff = 0.5 * (coeff[:, 0] + coeff[:, 1])
    position = lax.broadcasted_iota(jnp.int32, coeff.shape, 0) + base // 4
    w2[...] = jnp.where((position >= 0) & (position < total // 4), damping / (coeff + 4.125), 0.0).reshape(w2.shape)

    def node(ref, layer, r, fine):
        return ref[pl.ds(layer * (R if fine else SUB) + r, 1), :]

    def rows(ref, layer, t):
        return [ref[layer * R + r, pl.ds(t * SUB, SUB), :] for r in range(R)]

    def put(ref, layer, t, values):
        for r in range(R):
            ref[layer * R + r, pl.ds(t * SUB, SUB), :] = values[r]

    cases = tiles * SUB
    to = lax.broadcasted_iota(jnp.int32, (lanes, lanes), 0)
    fro = lax.broadcasted_iota(jnp.int32, (lanes, lanes), 1)
    step_apart = ((to - fro) % lanes == 1) | ((fro - to) % lanes == 1)
    ring[...] = jnp.where(step_apart, 1.0, 0.0).astype(bf16)

    def beside(x):
        flat = x.reshape(-1, lanes)
        top = flat.astype(bf16)
        rest = (flat - top.astype(f32)).astype(bf16)
        both = jnp.concatenate([top, rest], axis=1)
        two = jnp.concatenate([ring[...], ring[...]], axis=0)
        return jnp.dot(both, two, preferred_element_type=f32).reshape(x.shape)

    def block(ref, layer, count):
        return ref[pl.ds(layer * R, count * R)]

    def neighbours(src, layer, count, weight):
        by_matrix = [(i, r) for i in range(count) for r in range(R) if r % 2 == 0]
        flat = [src[(layer + i) * R + r] for i, r in by_matrix]
        got = beside(jnp.concatenate(flat, axis=0))
        side = {key: got[j * cases : (j + 1) * cases] for j, key in enumerate(by_matrix)}
        out = []
        for i in range(count):
            line = []
            for r in range(R):
                axial = src[(layer + i - 1) * R + r] + src[(layer + i + 1) * R + r]
                if weight != 1.0:
                    axial = weight * axial
                if (i, r) in side:
                    beside_it = side[i, r]
                else:
                    here = src[(layer + i) * R + r]
                    beside_it = jnp.concatenate([pltpu.roll(here[q * SUB : (q + 1) * SUB], 1, 1) + pltpu.roll(here[q * SUB : (q + 1) * SUB], lanes - 1, 1) for q in range(tiles)], axis=0)
                x = axial + beside_it
                if r > 0:
                    x = x + src[(layer + i) * R + r - 1]
                if r < R - 1:
                    x = x + src[(layer + i) * R + r + 1]
                line.append(x)
            out.append(line)
        return out

    def sweep(src, dst, b, w, lo, hi, weight, fine, step=8):
        def body(layer, count):
            nv = neighbours(src, layer, count, weight)
            for i in range(count):
                for r in range(R):
                    row = (layer + i) * R + r
                    dst[row] = (1.0 - damping) * src[row] + node(w, layer + i, r, fine) * (b[row] + nv[i][r])

        over(lo, hi, step, body)

    pair = 2 * lanes
    wide = quads // 2
    for h in range(wide):
        both = jnp.concatenate([jnp.concatenate([table[t * quads + 2 * h], table[t * quads + 2 * h + 1]], axis=1) for t in range(tiles)], axis=0)
        top = both.astype(bf16)
        stack[pl.ds(2 * h * cases, cases), :] = top
        stack[pl.ds((2 * h + 1) * cases, cases), :] = (both - top.astype(f32)).astype(bf16)

    def by_matrix(index):
        spot = lax.broadcasted_iota(jnp.int16, (pair, lanes), 0)
        place = jnp.broadcast_to(index & (pair - 1), (2 * SUB, lanes)).astype(jnp.int16)
        place = jnp.concatenate([place] * (pair // (2 * SUB)), axis=0)
        hot = jnp.where(spot == place, jnp.ones((), bf16), jnp.zeros((), bf16))
        got = jnp.dot(stack[...], hot, preferred_element_type=f32)
        value = got[:cases] + got[cases : 2 * cases]
        for h in range(1, wide):
            value = jnp.where(jnp.broadcast_to(index, value.shape) >= h * pair, got[2 * h * cases : (2 * h + 1) * cases] + got[(2 * h + 1) * cases : (2 * h + 2) * cases], value)
        return value

    def by_lanes(index):
        wide_index = jnp.broadcast_to(index, (SUB, lanes))
        low = jnp.broadcast_to(index & (lanes - 1), (SUB, lanes))
        beyond = [wide_index >= q * lanes for q in range(1, quads)]
        out = []
        for t in range(tiles):
            value = jnp.take_along_axis(table[t * quads], low, axis=1)
            for q in range(1, quads):
                value = jnp.where(beyond[q - 1], jnp.take_along_axis(table[t * quads + q], low, axis=1), value)
            out.append(value)
        return jnp.concatenate(out, axis=0)

    def loads(layer, count):
        for i in range(count):
            for r in range(R):
                index = node(picked, layer + i, r, True)
                value = by_matrix(index) if r % 2 else by_lanes(index)
                value = value * node(scale, layer + i, r, True)
                b0[(layer + i) * R + r] = value
                va[(layer + i) * R + r] = value * node(w0, layer + i, r, True)

    def residual(src, b, d, layer, count, weight, fine):
        nv = neighbours(src, layer, count, weight)
        return [[b[(layer + i) * R + r] - node(d, layer + i, r, fine) * src[(layer + i) * R + r] + nv[i][r]
                 for r in range(R)] for i in range(count)]

    def restrict(src, b, d, weight, fine, coarse_b, coarse_v, w, lo, hi, start, step):
        first = residual(src, b, d, 2 * lo - 1, 1, weight, fine)[0]
        for r in range(R):
            kept[r] = first[r]

        def body(layer, count):
            f = residual(src, b, d, 2 * layer, 2 * count, weight, fine)
            for i in range(count):
                lead = jnp.where(layer + i + start > 0, 0.25, 0.0).astype(f32)
                for r in range(R):
                    before = kept[r] if i == 0 else f[2 * i - 1][r]
                    value = 0.5 * f[2 * i][r] + (0.25 * f[2 * i + 1][r] + lead * before)
                    row = (layer + i) * R + r
                    coarse_b[row] = value
                    coarse_v[row] = value * node(w, layer + i, r, False)
            for r in range(R):
                kept[r] = f[-1][r]

        over(lo, hi, step, body)

    def prolong(coarse, fine, lo, hi, start, step=4):
        def body(layer, count):
            for t in range(tiles):
                c = [rows(coarse, layer + i, t) for i in range(count + 1)]
                for i in range(count):
                    half = jnp.where(layer + i + start >= 0, 0.5, 0.0).astype(f32)
                    v = rows(fine, 2 * (layer + i), t)
                    put(fine, 2 * (layer + i), t, [v[r] + c[i][r] for r in range(R)])
                    v = rows(fine, 2 * (layer + i) + 1, t)
                    put(fine, 2 * (layer + i) + 1, t, [v[r] + half * (c[i][r] + c[i + 1][r]) for r in range(R)])

        over(lo, hi, step, body)

    first, last = REACH - BELOW, REACH + n - 1 + ABOVE
    over(first, last, 18, loads)
    sweep(va, vb, b0, w0, first + 1, last - 1, 1.0, True, 23)
    mid, half = REACH // 2, n // 2
    restrict(vb, b0, d0, 1.0, True, b1, xa, w1, mid - 13, mid + half + 13, base // 2, 11)
    sweep(xa, xb, b1, w1, mid - 12, mid + half + 12, 0.25, False, 16)
    low_mid, quarter = REACH // 4, n // 4
    restrict(xb, b1, d1, 0.25, False, b2, ya, w2, low_mid - 5, low_mid + quarter + 5, base // 4, 14)
    sweep(ya, yb, b2, w2, low_mid - 4, low_mid + quarter + 4, 0.0625, False, 12)
    sweep(yb, ya, b2, w2, low_mid - 3, low_mid + quarter + 3, 0.0625, False, 12)
    sweep(ya, yb, b2, w2, low_mid - 2, low_mid + quarter + 2, 0.0625, False, 12)
    prolong(yb, xb, low_mid - 2, low_mid + quarter + 1, base // 4, 7)
    sweep(xb, xa, b1, w1, mid - 3, mid + half + 2, 0.25, False, 12)
    sweep(xa, xb, b1, w1, mid - 2, mid + half + 1, 0.25, False, 12)
    prolong(xb, vb, mid - 2, mid + half + 1, base // 2, 9)
    sweep(vb, va, b0, w0, REACH - 2, REACH + n + 1, 1.0, True, 16)
    sweep(va, vb, b0, w0, REACH - 1, REACH + n, 1.0, True, 16)

    own = own_tiles * SUB

    def finish(layer, count):
        nv = neighbours(vb, layer, count, 1.0)
        for i in range(count):
            for r in range(R):
                at = (layer + i) * R + r
                row = (layer + i - REACH) * R + r
                here = vb[at]
                if row < split:
                    first_out[row] = here
                else:
                    second_out[row - split] = here
                image = node(d0, layer + i, r, True) * here - nv[i][r]
                load = b0[at]
                def mine_of(x):
                    return jnp.where(own_slot == 0, x[:own], x[own:])
                field_out[:, row, :] = mine_of(here)
                left_out[row, pl.ds(0, own), :] = mine_of(image)
                left_out[row, pl.ds(own, own), :] = mine_of(load)

    over(REACH, REACH + n - 1, 12, finish)


def cycle(table, block, mine, theirs, cases, own, n, total, R):
    hops = len(mine)
    extent = n + 2 * REACH
    lanes = table.shape[2]

    def field(layers):
        return pltpu.VMEM((layers * R, cases, lanes), f32)

    def coefficients(rows, dtype=f32):
        return pltpu.VMEM((rows, lanes), dtype)

    fine, middle, coarse = extent * R, extent // 2 * SUB, extent // 4 * SUB
    scratch = [
        pltpu.VMEM((3, fine // SUB, SUB, lanes), f32),
        coefficients(fine, jnp.int32),
        *(coefficients(rows) for rows in (fine, fine, fine, middle, middle, coarse)),
        *(field(extent) for _ in range(3)),
        *(field(extent // 2) for _ in range(3)),
        *(field(extent // 4) for _ in range(3)),
        field(1),
        pltpu.VMEM((lanes, lanes), bf16),
        pltpu.VMEM((cases * table.shape[0] * SUB // cases, 2 * lanes), bf16),
    ]
    vmem = pl.BlockSpec(memory_space=pltpu.VMEM)
    return pl.pallas_call(
        functools.partial(cycle_kernel, tiles=cases // SUB, own_tiles=own // SUB, n=n, total=total, R=R, hops=hops),
        out_shape=(
            jax.ShapeDtypeStruct((own, n * R, lanes), f32),
            jax.ShapeDtypeStruct((n * R // 2, cases, lanes), f32),
            jax.ShapeDtypeStruct((n * R // 2, cases, lanes), f32),
            jax.ShapeDtypeStruct((n * R, 2 * own, lanes), f32),
        ),
        in_specs=[vmem] * (2 + 2 * hops),
        out_specs=[vmem] * 4,
        scratch_shapes=scratch,
        compiler_params=pltpu.CompilerParams(vmem_limit_bytes=48 * 2**20),
    )(table, block, *mine, *theirs)


def halves(x):
    top = x.astype(bf16)
    return top, (x - top.astype(f32)).astype(bf16)


def partial_products(left, right, together=12):
    rows = right.shape[0]
    total = 0.0
    for i in range(0, rows, together):
        a = jnp.concatenate([left[i + j] for j in range(together)], axis=1)
        b = jnp.concatenate([right[i + j] for j in range(together)], axis=1)
        a_top, a_rest = halves(a)
        b_top, b_rest = halves(b)

        def dot(x, y):
            return lax.dot_general(x, y, (((1,), (1,)), ((), ())), preferred_element_type=f32)

        both = dot(jnp.concatenate([a_top, a_rest], axis=0), b_top)
        total = total + (both[: a.shape[0]] + (both[a.shape[0] :] + dot(a_top, b_rest)))
    return total


def near_kernel(left, first, second, out):
    split = first.shape[0]
    out[...] = partial_products(left, first) + partial_products(left.at[pl.ds(split, split)], second)


def early_kernel(left, first, out):
    out[...] = partial_products(left, first)


def late_kernel(left, second, near, early, odd_group, out, *, own):
    split = second.shape[0]
    here, other = near[...], early[...] + partial_products(left.at[pl.ds(split, split)], second)
    even_group = odd_group[...] == 0
    even, odd = jnp.where(even_group, here, other), jnp.where(even_group, other, here)
    parts = []
    for q in range(here.shape[1] // own):
        parts += [even[:, q * own : (q + 1) * own], odd[:, q * own : (q + 1) * own]]
    out[...] = jnp.concatenate(parts, axis=1)


def product_call(kernel, shape, macs, *operands):
    vmem = pl.BlockSpec(memory_space=pltpu.VMEM)
    return pl.pallas_call(
        kernel,
        out_shape=jax.ShapeDtypeStruct(shape, f32),
        in_specs=[vmem] * len(operands),
        out_specs=vmem,
        cost_estimate=pl.CostEstimate(flops=6 * macs, bytes_accessed=4 * sum(x.size for x in operands), transcendentals=0),
        compiler_params=pltpu.CompilerParams(vmem_limit_bytes=32 * 2**20),
    )(*operands)


def pack_kernel(panel, flags, diagonal, out):
    for which, x in enumerate((panel, flags, diagonal)):
        out[which] = x[...].astype(f32)


def pack(panel, flags, diagonal):
    vmem = pl.BlockSpec(memory_space=pltpu.VMEM)
    return pl.pallas_call(
        pack_kernel,
        out_shape=jax.ShapeDtypeStruct((3, *panel.shape), f32),
        in_specs=[vmem] * 3,
        out_specs=vmem,
    )(panel, flags, diagonal)


def sum_over_slabs(x):
    count = lax.axis_size("slab")
    if count & (count - 1):
        return lax.psum(x, "slab")
    by = 1
    while by < count:
        x = x + lax.ppermute(x, "slab", [(i, i ^ by) for i in range(count)])
        by *= 2
    return x


def local(pressure, panel, flags, diagonal):
    n, R, lanes = panel.shape
    slabs, groups = lax.axis_size("slab"), lax.axis_size("case")
    own = pressure.shape[0] // groups
    slots = groups // 2
    cases = own * slots
    total = n * slabs
    group = lax.axis_index("case")

    per = SUB // R
    packed = [x.reshape(n // per, SUB, lanes) for x in (panel, flags, diagonal)]
    block = pack(*packed)
    hops = -(-REACH // n)
    mine = []
    for k in range(1, hops + 1):
        pairs = []
        for s in range(slabs):
            for g in range(groups):
                to = s + k if g % 2 == 0 else s - k
                pairs.append((s * groups + g, to * groups + g if 0 <= to < slabs else s * groups + (g ^ 1)))
        mine.append(lax.ppermute(block, ("slab", "case"), pairs))
    swap = [(g, g ^ 1) for g in range(groups)]
    theirs = [lax.ppermute(x, "case", swap) for x in mine]

    table = pressure.reshape(slots, 2, own // SUB, SUB, -1, lanes)
    table = lax.dynamic_index_in_dim(table, group % 2, 1, keepdims=False)
    table = table.swapaxes(2, 3).reshape(-1, SUB, lanes)

    fields, first, second, left = cycle(table, block, mine, theirs, cases, own, n, total, R)
    first_there = lax.ppermute(first, "case", swap)
    second_there = lax.ppermute(second, "case", swap)
    part = (2 * own, cases)
    macs = 2 * own * first.size
    near = product_call(near_kernel, part, 2 * macs, left, first, second)
    early = product_call(early_kernel, part, macs, left, first_there)
    late = functools.partial(late_kernel, own=own)
    odd_group = jnp.broadcast_to(group % 2, part).astype(jnp.int32)
    products = product_call(late, (2 * own, 2 * cases), macs, left, second_there, near, early, odd_group)
    sums = sum_over_slabs(products)
    sums = sums * (1.0 / (total * R * lanes))
    return fields.reshape(own, n, R, lanes), sums[:own], sums[own:]


def solution(mesh):
    in_specs = (P(), P("slab", None, None), P("slab", None, None), P("slab", None, None))
    out_specs = (P("case", "slab", None, None), P("case", None), P("case", None))
    return jax.shard_map(local, mesh=mesh, in_specs=in_specs, out_specs=out_specs, check_vma=False)
```
